32 devices in a mesh: rep: 4 (over z), fsdp: 8 (over y, x, core).
Axes of the slice: x: 2, y: 2, z: 4, core: 2. Of those that a mesh axis runs over, the one named last changes fastest.
Arguments:
- grads: bfloat16 [4, 8, 768, 2048], P('rep', None, 'fsdp'), may hold values from -400 to 400
- momentum: float32 [8, 8, 96, 2048], P('fsdp', None, 'rep'), may hold values from -384 to 384
- owner: int32 [8], replicated, may hold values from 0 to 7, each once
Outputs:
- update: bfloat16 [8, 8, 96, 2048], P(None, 'fsdp', 'rep')
- momentum_out: float32 [8, 8, 96, 2048], P('fsdp', None, 'rep')
The draws below stay inside these ranges and needn't reach their ends.
Inputs may be any that keep to these rules, and one draw needn't show every extreme that they name: `owner`: every slot holds exactly one expert.
All inputs are finite; a program needn't handle non-finite values.
Results may differ from the reference program's by a relative error of at most 0.012.
Values may be sent and summed in bfloat16 or wider, within the bound.
A program may use at most 64 MiB of HBM per device.

```python
import math
import jax
import jax.numpy as jnp
from jax import lax

D = 2048
FF = 768
ITERS = 2
EXPERTS = 8
REPLICAS = 4
BLOCKS = 8
SHARD_ROWS = 96


def draw_grads(key, part):
    key_noise, key_rows, key_cols = jax.random.split(jax.random.fold_in(key, 11), 3)
    row_scale = jnp.exp(jax.random.uniform(key_rows, (1, EXPERTS, FF, 1), jnp.float32, 0.0, math.log(10.0)))
    col_scale = jnp.exp(jax.random.uniform(key_cols, (1, EXPERTS, 1, D), jnp.float32, 0.0, math.log(10.0)))
    noise = jnp.clip(jax.random.normal(key_noise, (REPLICAS, EXPERTS, FF, D), jnp.float32), -4.0, 4.0)
    values = noise * row_scale * col_scale
    return jnp.clip(values, -400.0, 400.0).astype(jnp.bfloat16)


def block_levels(key, dims, shards, low, top_value):
    factor_of = 1.0
    for dim, parts in shards:
        draws = jax.random.uniform(jax.random.fold_in(jax.random.fold_in(key, 6), dim), (parts,), jnp.float32, low / len(shards), top_value / len(shards))
        factor_of = factor_of * jnp.repeat(jnp.exp(draws), dims[dim] // parts).reshape((-1,) + (1,) * (len(dims) - 1 - dim))
    return factor_of


def centred(key, dims, deviation, bound, cuts=(), kind=jnp.bfloat16):
    drawn = deviation * jax.random.normal(key, dims, jnp.float32)
    if cuts:
        drawn = drawn * block_levels(key, dims, cuts, -0.22, 0.18)
    return jnp.clip(drawn, -bound, bound).astype(kind)


def setup_inputs(seed: int = 0) -> dict:
    keys = jax.random.split(jax.random.key(seed), 4)
    return {
        "grads": draw_grads(jax.random.fold_in(keys[3], 71), 0),
        "momentum": centred(keys[1], (EXPERTS, BLOCKS, SHARD_ROWS, D), 60.0, 384.0, ((0, 8), (2, 4)), jnp.float32),
        "owner": jax.random.permutation(keys[2], EXPERTS).astype(jnp.int32),
    }


DECAY_RATE = 0.95
NEWTON_A = 3.4445
NEWTON_B = -4.775
NEWTON_C = 2.0315
EPSILON = 1e-07

def newton(nesterov):
    values = nesterov.astype(jnp.float32)
    frobenius = jnp.sqrt(jnp.sum(values * values))
    iterate = (values / (frobenius + EPSILON)).astype(jnp.bfloat16)
    result = values
    for iteration in range(ITERS):
        gram_matrix = jnp.dot(iterate, iterate.T, preferred_element_type=jnp.float32).astype(jnp.bfloat16)
        squared = jnp.dot(gram_matrix, gram_matrix, preferred_element_type=jnp.float32)
        polynomial = (NEWTON_B * gram_matrix.astype(jnp.float32) + NEWTON_C * squared).astype(jnp.bfloat16)
        result = NEWTON_A * iterate.astype(jnp.float32) + jnp.dot(polynomial, iterate, preferred_element_type=jnp.float32)
        iterate = result.astype(jnp.bfloat16)
    return result

def reference(grads, momentum, owner):
    full_moment = momentum.reshape(EXPERTS, FF, D)
    factor = math.sqrt(D)

    def one_expert(expert):
        replicas = lax.dynamic_index_in_dim(grads, expert, 1, keepdims=False)
        total = lax.optimization_barrier(jnp.sum(replicas.astype(jnp.float32), axis=0))
        slot = owner[expert]
        moment = lax.dynamic_index_in_dim(full_moment, slot, 0, keepdims=False)
        moment_new = DECAY_RATE * moment + total
        nesterov = (total + DECAY_RATE * moment_new).astype(jnp.bfloat16)
        update = (factor * newton(nesterov)).astype(jnp.bfloat16)
        return (update, moment_new)
    updates, moments = lax.map(one_expert, jnp.arange(EXPERTS, dtype=jnp.int32))
    moment_out = jnp.zeros((EXPERTS, FF, D), jnp.float32).at[owner].set(moments)
    return (updates.reshape(EXPERTS, BLOCKS, SHARD_ROWS, D), moment_out.reshape(EXPERTS, BLOCKS, SHARD_ROWS, D))
```

```python
import functools
import math

import jax
import jax.numpy as jnp
from jax import lax
from jax.experimental import pallas as pl
from jax.experimental.pallas import tpu as pltpu
from jax.sharding import PartitionSpec as P

ITERS = 2
CHUNKS = 4


DECAY_RATE = 0.95
NEWTON_A = 3.4445
NEWTON_B = -4.775
NEWTON_C = 2.0315
EPSILON = 1e-07
MESH = pl.DeviceIdType.MESH
F32 = jnp.float32
BF16 = jnp.bfloat16


def dot(left, right):
    return jnp.dot(left, right, preferred_element_type=F32)


def fold(block):
    half = block.shape[1] // 2
    return jnp.concatenate([block[:, :half], block[:, half:]], axis=0)


def unfold(block):
    half = block.shape[0] // 2
    return jnp.concatenate([block[:half], block[half:]], axis=1)


def step_kernel(
    Z, F, C,
    owner_ref, grads_ref, mom_ref,
    upd_ref, mout_ref,
    g32, sbuf, rbuf, asend, arecv, nall, gacc, gb, pb, g2b, wb, tsend,
    rs_s, rs_r, a_s, a_r, ag_s, ag_r, t_s, t_r, *trecv,
):
    r = lax.axis_index("rep")
    f = lax.axis_index("fsdp")
    q, width = mom_ref.shape[2], mom_ref.shape[3]
    cc = width // C
    rows = F * q
    ff = Z * rows
    last = Z - 1

    barrier = pltpu.get_barrier_semaphore()

    @pl.when(r > 0)
    def _():
        pl.semaphore_signal(barrier, inc=1, device_id={"rep": r - 1}, device_id_type=MESH)

    @pl.when(r < last)
    def _():
        pl.semaphore_signal(barrier, inc=1, device_id={"rep": r + 1}, device_id_type=MESH)

    for k in range(1, F):
        pl.semaphore_signal(barrier, inc=1, device_id={"fsdp": lax.rem(f + k, F)}, device_id_type=MESH)

    owners = [owner_ref[e] for e in range(F)]
    expert_of = []
    for s in range(F):
        found = jnp.int32(0)
        for e in range(1, F):
            found = jnp.where(owners[e] == s, jnp.int32(e), found)
        expert_of.append(found)

    def cols(c):
        return pl.ds(c * cc, cc)

    def prepare(c):
        for s in range(F):
            block = grads_ref[0, expert_of[s], :, cols(c)].astype(F32)
            for d in range(Z):
                g32[d, s * q:(s + 1) * q, cols(c)] = block[d * q:(d + 1) * q]

    def position(way):
        return r if way == 0 else last - r

    def ahead(way, n):
        return r + n if way == 0 else r - n

    def rs_copy(c, way, t):
        return pltpu.make_async_remote_copy(
            src_ref=sbuf.at[way, c, t], dst_ref=rbuf.at[way, c, t],
            send_sem=rs_s.at[way, c, t], recv_sem=rs_r.at[way, c, t],
            device_id={"rep": ahead(way, 1)}, device_id_type=MESH)

    def reduce_slot(c, t):
        for way in range(2):
            pos = position(way)
            dest = ahead(way, last - t)
            if t > 0:
                @pl.when(jnp.logical_and(pos > 0, pos <= t))
                def _(way=way, dest=dest):
                    rs_copy(c, way, t - 1).wait_recv()
                    sbuf[way, c, t] = (g32[dest, :, cols(c)] + rbuf[way, c, t - 1].astype(F32)).astype(BF16)
                    rs_copy(c, way, t).start()

            @pl.when(pos == 0)
            def _(way=way, dest=dest):
                sbuf[way, c, t] = g32[dest, :, cols(c)].astype(BF16)
                rs_copy(c, way, t).start()

    def a_copy(c, k):
        peer = lax.rem(f + k, F)
        return pltpu.make_async_remote_copy(
            src_ref=asend.at[c, peer], dst_ref=arecv.at[c, f],
            send_sem=a_s.at[c, k], recv_sem=a_r.at[c, k],
            device_id={"fsdp": peer}, device_id_type=MESH)

    def a_arrival(c, k):
        peer = lax.rem(f + F - k, F)
        return pltpu.make_async_remote_copy(
            src_ref=asend.at[c, peer], dst_ref=arecv.at[c, peer],
            send_sem=a_s.at[c, k], recv_sem=a_r.at[c, k],
            device_id={"fsdp": peer}, device_id_type=MESH)

    def reduce_last(c):
        for way in range(2):
            @pl.when(position(way) > 0)
            def _(way=way):
                rs_copy(c, way, last - 1).wait_recv()
                g32[r, :, cols(c)] += rbuf[way, c, last - 1].astype(F32)
        for s in range(F):
            asend[c, s] = fold(g32[r, s * q:(s + 1) * q, cols(c)]).astype(BF16)
        for k in range(1, F):
            a_copy(c, k).start()
        arecv[c, f] = asend[c, f]

    def own_copy(c, way):
        return pltpu.make_async_remote_copy(
            src_ref=nall.at[c, r], dst_ref=nall.at[c, r],
            send_sem=ag_s.at[way, c, 0], recv_sem=ag_r.at[way, c, 0],
            device_id={"rep": ahead(way, 1)}, device_id_type=MESH)

    def pass_copy(c, way, k):
        source = ahead(way, -1 - k)
        return pltpu.make_async_remote_copy(
            src_ref=nall.at[c, source], dst_ref=nall.at[c, source],
            send_sem=ag_s.at[way, c, k + 1], recv_sem=ag_r.at[way, c, k + 1],
            device_id={"rep": ahead(way, 1)}, device_id_type=MESH)

    def gather_arrival(c, way, k):
        source = ahead(way, -1 - k)
        return pltpu.make_async_remote_copy(
            src_ref=nall.at[c, source], dst_ref=nall.at[c, source],
            send_sem=ag_s.at[way, c, k], recv_sem=ag_r.at[way, c, k],
            device_id={"rep": ahead(way, -1)}, device_id_type=MESH)

    def momentum_rows(c):
        for k in range(1, F):
            a_arrival(c, k).wait_recv()
        for pair in range(F // 2):
            parts = []
            for b in (2 * pair, 2 * pair + 1):
                total = unfold(arecv[c, b].astype(F32))
                moved = DECAY_RATE * mom_ref[0, b, :, cols(c)] + total
                mout_ref[0, b, :, cols(c)] = moved
                parts.append(total + DECAY_RATE * moved)
            nall[c, r, 2 * pair * q:(2 * pair + 2) * q] = jnp.concatenate(parts, axis=0).astype(BF16)
        for way in range(2):
            @pl.when(position(way) < last)
            def _(way=way):
                own_copy(c, way).start()

    def gather_slot(c, k):
        for way in range(2):
            pos = position(way)

            @pl.when(pos > k)
            def _(way=way):
                gather_arrival(c, way, k).wait_recv()

            if k + 1 < last:
                @pl.when(jnp.logical_and(pos > k, pos < last))
                def _(way=way):
                    pass_copy(c, way, k).start()

    def row_blocks(body):
        size = ff // 2

        def step(i, carry):
            body(pl.ds(pl.multiple_of(i * size, size), size), i * size)
            return carry

        lax.fori_loop(0, 2, step, 0)

    def gram(c):
        whole = nall[c].reshape(ff, cc)
        half = Z // 2

        def step(i, carry):
            mine = nall[c, pl.ds(i * half, half)].reshape(half * rows, cc)
            part = lax.dot_general(mine, whole, (((1,), (1,)), ((), ())), preferred_element_type=F32)
            at = pl.ds(pl.multiple_of(i * half * rows, half * rows), half * rows)
            if c == 0:
                gacc[at, :] = part
            else:
                gacc[at, :] += part
            return carry

        lax.fori_loop(0, 2, step, 0)

    prepare(0)
    pl.semaphore_wait(barrier, (F - 1) + (r > 0).astype(jnp.int32) + (r < last).astype(jnp.int32))
    reduce_slot(0, 0)
    for c in range(C):
        if c + 1 < C:
            prepare(c + 1)
        for t in range(1, last):
            reduce_slot(c, t)
            if c > 0:
                gather_slot(c - 1, t - 1)
        if c + 1 < C:
            reduce_slot(c + 1, 0)
        reduce_last(c)
        if c > 0:
            gather_slot(c - 1, last - 1)
            gram(c - 1)
        momentum_rows(c)
    for k in range(last):
        gather_slot(C - 1, k)
    gram(C - 1)

    trace = jnp.zeros((1, 1), F32)
    size = ff // 2
    for i in range(2):
        at = slice(i * size, (i + 1) * size)
        row = lax.broadcasted_iota(jnp.int32, (size, size), 0)
        col = lax.broadcasted_iota(jnp.int32, (size, size), 1)
        trace += jnp.sum(jnp.where(row == col, gacc[at, at], 0.0), keepdims=True)
    scale = 1.0 / (jnp.sqrt(trace) + EPSILON)

    def normalise(at, _):
        scaled = gacc[at, :] * (scale * scale)
        gacc[at, :] = scaled
        gb[at, :] = scaled.astype(BF16)

    row_blocks(normalise)

    def first_polynomial(at, _):
        mine = gb[at, :]
        pb[at, :] = (NEWTON_B * mine.astype(F32) + NEWTON_C * dot(mine, gb[...])).astype(BF16)

    row_blocks(first_polynomial)

    def second_gram(at, _):
        mixed = dot(pb[at, :], gb[...])
        outer = dot(mixed.astype(BF16), pb[...])
        g2b[at, :] = (NEWTON_A * NEWTON_A * gacc[at, :] + 2.0 * NEWTON_A * mixed + outer).astype(BF16)

    row_blocks(second_gram)

    own = pl.ds(pl.multiple_of(r * rows, rows), rows)
    mine = g2b[own, :]
    second = (NEWTON_B * mine.astype(F32) + NEWTON_C * dot(mine, g2b[...])).astype(BF16)
    wb[...] = (
        NEWTON_A * (second.astype(F32) + pb[own, :].astype(F32)) + dot(second, pb[...])
    ).astype(BF16)

    def t_copy(c, k):
        peer = lax.rem(f + k, F)
        return pltpu.make_async_remote_copy(
            src_ref=tsend.at[c, peer], dst_ref=trecv[c].at[f],
            send_sem=t_s.at[c, k], recv_sem=t_r.at[c, k],
            device_id={"fsdp": peer}, device_id_type=MESH)

    def t_arrival(c, k):
        peer = lax.rem(f + F - k, F)
        return pltpu.make_async_remote_copy(
            src_ref=tsend.at[c, peer], dst_ref=trecv[c].at[peer],
            send_sem=t_s.at[c, k], recv_sem=t_r.at[c, k],
            device_id={"fsdp": peer}, device_id_type=MESH)

    factor = scale * math.sqrt(width)
    for c in range(C):
        product = dot(wb[...], nall[c].reshape(ff, cc))
        result = factor * (NEWTON_A * NEWTON_A * nall[c, r].astype(F32) + product)
        for b in range(F):
            tsend[c, b] = fold(result[b * q:(b + 1) * q]).astype(BF16)
        for k in range(1, F):
            t_copy(c, k).start()
        trecv[c][f] = tsend[c, f]

    for c in range(C):
        for k in range(1, F):
            t_arrival(c, k).wait_recv()
        for e in range(F):
            upd_ref[e, 0, :, cols(c)] = unfold(trecv[c][owners[e]].astype(F32)).astype(BF16)

    for c in range(C):
        for way in range(2):
            pos = position(way)
            for t in range(last):
                @pl.when(pos <= t)
                def _(c=c, way=way, t=t):
                    rs_copy(c, way, t).wait_send()

            @pl.when(pos < last)
            def _(c=c, way=way):
                own_copy(c, way).wait_send()

            for k in range(last - 1):
                @pl.when(jnp.logical_and(pos > k, pos < last))
                def _(c=c, way=way, k=k):
                    pass_copy(c, way, k).wait_send()
        for k in range(1, F):
            a_copy(c, k).wait_send()
            t_copy(c, k).wait_send()


def fused_step(grads, momentum, owner):
    Z, F = lax.axis_size("rep"), lax.axis_size("fsdp")
    q, width = momentum.shape[2], momentum.shape[3]
    C = CHUNKS
    cc = width // C
    rows = F * q
    ff = Z * rows
    vmem = pl.BlockSpec(memory_space=pltpu.VMEM)
    dma = pltpu.SemaphoreType.DMA
    return pl.pallas_call(
        functools.partial(step_kernel, Z, F, C),
        out_shape=(
            jax.ShapeDtypeStruct((F, 1, q, width), BF16),
            jax.ShapeDtypeStruct(momentum.shape, F32),
        ),
        in_specs=[pl.BlockSpec(memory_space=pltpu.SMEM), vmem, vmem],
        out_specs=(vmem, vmem),
        scratch_shapes=[
            pltpu.VMEM((Z, rows, width), F32),
            pltpu.VMEM((2, C, Z - 1, rows, cc), BF16),
            pltpu.VMEM((2, C, Z - 1, rows, cc), BF16),
            pltpu.VMEM((C, F, 2 * q, cc // 2), BF16),
            pltpu.VMEM((C, F, 2 * q, cc // 2), BF16),
            pltpu.VMEM((C, Z, rows, cc), BF16),
            pltpu.VMEM((ff, ff), F32),
            pltpu.VMEM((ff, ff), BF16),
            pltpu.VMEM((ff, ff), BF16),
            pltpu.VMEM((ff, ff), BF16),
            pltpu.VMEM((rows, ff), BF16),
            pltpu.VMEM((C, F, 2 * q, cc // 2), BF16),
            dma((2, C, Z - 1)),
            dma((2, C, Z - 1)),
            dma((C, F)),
            dma((C, F)),
            dma((2, C, Z - 1)),
            dma((2, C, Z - 1)),
            dma((C, F)),
            dma((C, F)),
        ] + [pltpu.VMEM((F, 2 * q, cc // 2), BF16)] * C,
        compiler_params=pltpu.CompilerParams(
            collective_id=0, has_side_effects=True, vmem_limit_bytes=58 * 1024 * 1024
        ),
        cost_estimate=pl.CostEstimate(
            flops=2 * ff * ff * width, bytes_accessed=16 * rows * width, transcendentals=0
        ),
    )(owner, grads, momentum)


def finish_rows(own_gram, gram_matrix):
    squared = jnp.dot(own_gram, gram_matrix, preferred_element_type=jnp.float32)
    polynomial = (NEWTON_B * own_gram.astype(jnp.float32) + NEWTON_C * squared).astype(jnp.bfloat16)
    return polynomial


def rows_whole(current, first_row):
    slab_rows = current.shape[0]
    result = current.astype(jnp.float32)
    for iteration in range(ITERS):
        gathered = lax.all_gather(current, "rep", axis=0, tiled=True)
        if iteration == 0:
            values = gathered.astype(jnp.float32)
            frobenius = jnp.sqrt(jnp.sum(values * values))
            whole = (values / (frobenius + EPSILON)).astype(jnp.bfloat16)
            mine = lax.dynamic_slice_in_dim(whole, first_row, slab_rows, 0)
        else:
            whole = gathered
            mine = current
        gram_matrix = lax.dot_general(
            whole, whole, (((1,), (1,)), ((), ())), preferred_element_type=jnp.float32
        ).astype(jnp.bfloat16)
        own_gram = lax.dynamic_slice_in_dim(gram_matrix, first_row, slab_rows, 0)
        polynomial = finish_rows(own_gram, gram_matrix)
        result = NEWTON_A * mine.astype(jnp.float32) + jnp.dot(
            polynomial, whole, preferred_element_type=jnp.float32
        )
        current = result.astype(jnp.bfloat16)
    return result


def on_device(grads, momentum, owner):
    slots = lax.axis_size("fsdp")
    replica = lax.axis_index("rep")
    width = grads.shape[-1]
    terms = grads[0].astype(jnp.float32)
    summed = lax.psum_scatter(terms, "rep", scatter_dimension=1, tiled=True)
    onehot = (owner[:, None] == jnp.arange(slots, dtype=jnp.int32)[None, :]).astype(jnp.float32)
    outgoing = jnp.einsum("es,eqd->sqd", onehot, summed, precision=lax.Precision.HIGHEST)
    arrived = lax.all_to_all(outgoing, "fsdp", split_axis=0, concat_axis=1, tiled=True)
    grad_rows = arrived[0]
    moment = momentum[0].reshape(-1, width)
    moment_new = DECAY_RATE * moment + grad_rows
    nesterov = (grad_rows + DECAY_RATE * moment_new).astype(jnp.bfloat16)
    slab_rows = nesterov.shape[0]
    first_row = replica * slab_rows
    result = rows_whole(nesterov, first_row)
    factor = math.sqrt(width)
    update_rows = (factor * result).astype(jnp.bfloat16)
    returning = lax.all_to_all(
        update_rows.reshape(slots, slab_rows // slots, width),
        "fsdp",
        split_axis=0,
        concat_axis=0,
        tiled=True,
    )
    updates = jnp.einsum(
        "es,sqd->eqd", onehot.astype(jnp.bfloat16), returning, preferred_element_type=jnp.float32
    ).astype(jnp.bfloat16)
    return (updates[:, None], moment_new.reshape(1, slots, slab_rows // slots, width))


def step(grads, momentum, owner):
    Z, F = lax.axis_size("rep"), lax.axis_size("fsdp")
    q, width = momentum.shape[2], momentum.shape[3]
    if q % 8 == 0 and F % 2 == 0 and Z % 2 == 0 and Z > 2 and width % (256 * CHUNKS) == 0:
        return fused_step(grads, momentum, owner)
    return on_device(grads, momentum, owner)


def solution(mesh):
    placed = (P("rep", None, "fsdp", None), P("fsdp", None, "rep", None), P())
    return jax.shard_map(
        step,
        mesh=mesh,
        in_specs=placed,
        out_specs=(P(None, "fsdp", "rep", None), P("fsdp", None, "rep", None)),
        check_vma=False,
    )
```

```python
import functools
import math

import jax
import jax.numpy as jnp
from jax import lax
from jax.experimental import pallas as pl
from jax.experimental.pallas import tpu as pltpu
from jax.sharding import PartitionSpec as P

ITERS = 2
CHUNKS = 8


DECAY_RATE = 0.95
NEWTON_A = 3.4445
NEWTON_B = -4.775
NEWTON_C = 2.0315
EPSILON = 1e-07
MESH = pl.DeviceIdType.MESH
F32 = jnp.float32
BF16 = jnp.bfloat16


def dot(left, right):
    return jnp.dot(left, right, preferred_element_type=F32)


def fold(block):
    half = block.shape[1] // 2
    return jnp.concatenate([block[:, :half], block[:, half:]], axis=0)


def unfold(block):
    half = block.shape[0] // 2
    return jnp.concatenate([block[:half], block[half:]], axis=1)


def schedule(Z, C):
    start, stride, exchange = 0.34, 0.65, 0.57
    stages = [(0.0, "prepare", 0)]
    stages += [(start + stride * t, "reduce", t) for t in range(Z - 1)]
    owner = start + stride * (Z - 1)
    stages += [(owner, "owner", 0), (owner + exchange, "momentum", 0)]
    stages += [(owner + exchange + stride * (k + 1), "gather", k) for k in range(Z - 1)]
    stages += [(owner + exchange + stride * (Z - 1) + 0.1, "gram", 0)]
    order = sorted((c + at, stage, c, n) for c in range(C) for at, stage, n in stages)
    return [item[1:] for item in order]


def step_kernel(
    Z, F, C,
    owner_ref, grads_ref, mom_ref,
    upd_ref, mout_ref,
    g32, sbuf, rbuf, asend, arecv, nall, gacc, gb, pb, g2b, wb, tsend,
    rs_s, rs_r, a_s, a_r, ag_s, ag_r, t_s, t_r, *trecv,
):
    r = lax.axis_index("rep")
    f = lax.axis_index("fsdp")
    q, width = mom_ref.shape[2], mom_ref.shape[3]
    cc = width // C
    rows = F * q
    ff = Z * rows
    last = Z - 1

    barrier = pltpu.get_barrier_semaphore()

    @pl.when(r > 0)
    def _():
        pl.semaphore_signal(barrier, inc=1, device_id={"rep": r - 1}, device_id_type=MESH)

    @pl.when(r < last)
    def _():
        pl.semaphore_signal(barrier, inc=1, device_id={"rep": r + 1}, device_id_type=MESH)

    for k in range(1, F):
        pl.semaphore_signal(barrier, inc=1, device_id={"fsdp": lax.rem(f + k, F)}, device_id_type=MESH)

    owners = [owner_ref[e] for e in range(F)]
    expert_of = []
    for s in range(F):
        found = jnp.int32(0)
        for e in range(1, F):
            found = jnp.where(owners[e] == s, jnp.int32(e), found)
        expert_of.append(found)

    def cols(c):
        return pl.ds(c * cc, cc)

    def prepare(c):
        for s in range(F):
            block = grads_ref[0, expert_of[s], :, cols(c)].astype(F32)
            for d in range(Z):
                g32[d, s * q:(s + 1) * q, cols(c)] = block[d * q:(d + 1) * q]

    def position(way):
        return r if way == 0 else last - r

    def ahead(way, n):
        return r + n if way == 0 else r - n

    def rs_copy(c, way, t):
        return pltpu.make_async_remote_copy(
            src_ref=sbuf.at[way, c, t], dst_ref=rbuf.at[way, c, t],
            send_sem=rs_s.at[way, c, t], recv_sem=rs_r.at[way, c, t],
            device_id={"rep": ahead(way, 1)}, device_id_type=MESH)

    def reduce_slot(c, t):
        for way in range(2):
            pos = position(way)
            dest = ahead(way, last - t)
            if t > 0:
                @pl.when(jnp.logical_and(pos > 0, pos <= t))
                def _(way=way, dest=dest):
                    rs_copy(c, way, t - 1).wait_recv()
                    sbuf[way, c, t] = (g32[dest, :, cols(c)] + rbuf[way, c, t - 1].astype(F32)).astype(BF16)
                    rs_copy(c, way, t).start()

            @pl.when(pos == 0)
            def _(way=way, dest=dest):
                sbuf[way, c, t] = g32[dest, :, cols(c)].astype(BF16)
                rs_copy(c, way, t).start()

    def a_copy(c, k):
        peer = lax.rem(f + k, F)
        return pltpu.make_async_remote_copy(
            src_ref=asend.at[c, peer], dst_ref=arecv.at[c, f],
            send_sem=a_s.at[c, k], recv_sem=a_r.at[c, k],
            device_id={"fsdp": peer}, device_id_type=MESH)

    def a_arrival(c, k):
        peer = lax.rem(f + F - k, F)
        return pltpu.make_async_remote_copy(
            src_ref=asend.at[c, peer], dst_ref=arecv.at[c, peer],
            send_sem=a_s.at[c, k], recv_sem=a_r.at[c, k],
            device_id={"fsdp": peer}, device_id_type=MESH)

    def reduce_last(c):
        for way in range(2):
            @pl.when(position(way) > 0)
            def _(way=way):
                rs_copy(c, way, last - 1).wait_recv()
                g32[r, :, cols(c)] += rbuf[way, c, last - 1].astype(F32)
        for s in range(F):
            asend[c, s] = fold(g32[r, s * q:(s + 1) * q, cols(c)]).astype(BF16)
        for k in range(1, F):
            a_copy(c, k).start()
        arecv[c, f] = asend[c, f]

    def own_copy(c, way):
        return pltpu.make_async_remote_copy(
            src_ref=nall.at[c, r], dst_ref=nall.at[c, r],
            send_sem=ag_s.at[way, c, 0], recv_sem=ag_r.at[way, c, 0],
            device_id={"rep": ahead(way, 1)}, device_id_type=MESH)

    def pass_copy(c, way, k):
        source = ahead(way, -1 - k)
        return pltpu.make_async_remote_copy(
            src_ref=nall.at[c, source], dst_ref=nall.at[c, source],
            send_sem=ag_s.at[way, c, k + 1], recv_sem=ag_r.at[way, c, k + 1],
            device_id={"rep": ahead(way, 1)}, device_id_type=MESH)

    def gather_arrival(c, way, k):
        source = ahead(way, -1 - k)
        return pltpu.make_async_remote_copy(
            src_ref=nall.at[c, source], dst_ref=nall.at[c, source],
            send_sem=ag_s.at[way, c, k], recv_sem=ag_r.at[way, c, k],
            device_id={"rep": ahead(way, -1)}, device_id_type=MESH)

    def momentum_rows(c):
        for k in range(1, F):
            a_arrival(c, k).wait_recv()
        for pair in range(F // 2):
            parts = []
            for b in (2 * pair, 2 * pair + 1):
                total = unfold(arecv[c, b].astype(F32))
                moved = DECAY_RATE * mom_ref[0, b, :, cols(c)] + total
                mout_ref[0, b, :, cols(c)] = moved
                parts.append(total + DECAY_RATE * moved)
            nall[c, r, 2 * pair * q:(2 * pair + 2) * q] = jnp.concatenate(parts, axis=0).astype(BF16)
        for way in range(2):
            @pl.when(position(way) < last)
            def _(way=way):
                own_copy(c, way).start()

    def gather_slot(c, k):
        for way in range(2):
            pos = position(way)

            @pl.when(pos > k)
            def _(way=way):
                gather_arrival(c, way, k).wait_recv()

            if k + 1 < last:
                @pl.when(jnp.logical_and(pos > k, pos < last))
                def _(way=way):
                    pass_copy(c, way, k).start()

    def row_blocks(body):
        size = ff // 2

        def step(i, carry):
            body(pl.ds(pl.multiple_of(i * size, size), size), i * size)
            return carry

        lax.fori_loop(0, 2, step, 0)

    def gram(c):
        whole = nall[c].reshape(ff, cc)
        half = Z // 2

        def step(i, carry):
            mine = nall[c, pl.ds(i * half, half)].reshape(half * rows, cc)
            part = lax.dot_general(mine, whole, (((1,), (1,)), ((), ())), preferred_element_type=F32)
            at = pl.ds(pl.multiple_of(i * half * rows, half * rows), half * rows)
            if c == 0:
                gacc[at, :] = part
            else:
                gacc[at, :] += part
            return carry

        lax.fori_loop(0, 2, step, 0)

    prepare(0)
    pl.semaphore_wait(barrier, (F - 1) + (r > 0).astype(jnp.int32) + (r < last).astype(jnp.int32))
    for stage, c, n in schedule(Z, C):
        if stage == "prepare" and c > 0:
            prepare(c)
        elif stage == "reduce":
            reduce_slot(c, n)
        elif stage == "owner":
            reduce_last(c)
        elif stage == "momentum":
            momentum_rows(c)
        elif stage == "gather":
            gather_slot(c, n)
        elif stage == "gram":
            gram(c)

    trace = jnp.zeros((1, 1), F32)
    size = ff // 2
    for i in range(2):
        at = slice(i * size, (i + 1) * size)
        row = lax.broadcasted_iota(jnp.int32, (size, size), 0)
        col = lax.broadcasted_iota(jnp.int32, (size, size), 1)
        trace += jnp.sum(jnp.where(row == col, gacc[at, at], 0.0), keepdims=True)
    scale = 1.0 / (jnp.sqrt(trace) + EPSILON)

    def normalise(at, _):
        scaled = gacc[at, :] * (scale * scale)
        gacc[at, :] = scaled
        gb[at, :] = scaled.astype(BF16)

    row_blocks(normalise)

    def first_polynomial(at, _):
        mine = gb[at, :]
        pb[at, :] = (NEWTON_B * mine.astype(F32) + NEWTON_C * dot(mine, gb[...])).astype(BF16)

    row_blocks(first_polynomial)

    def second_gram(at, _):
        mixed = dot(pb[at, :], gb[...])
        outer = dot(mixed.astype(BF16), pb[...])
        g2b[at, :] = (NEWTON_A * NEWTON_A * gacc[at, :] + 2.0 * NEWTON_A * mixed + outer).astype(BF16)

    row_blocks(second_gram)

    own = pl.ds(pl.multiple_of(r * rows, rows), rows)
    mine = g2b[own, :]
    second = (NEWTON_B * mine.astype(F32) + NEWTON_C * dot(mine, g2b[...])).astype(BF16)
    wb[...] = (
        NEWTON_A * (second.astype(F32) + pb[own, :].astype(F32)) + dot(second, pb[...])
    ).astype(BF16)

    def t_copy(c, k):
        peer = lax.rem(f + k, F)
        return pltpu.make_async_remote_copy(
            src_ref=tsend.at[c, peer], dst_ref=trecv[c].at[f],
            send_sem=t_s.at[c, k], recv_sem=t_r.at[c, k],
            device_id={"fsdp": peer}, device_id_type=MESH)

    def t_arrival(c, k):
        peer = lax.rem(f + F - k, F)
        return pltpu.make_async_remote_copy(
            src_ref=tsend.at[c, peer], dst_ref=trecv[c].at[peer],
            send_sem=t_s.at[c, k], recv_sem=t_r.at[c, k],
            device_id={"fsdp": peer}, device_id_type=MESH)

    factor = scale * math.sqrt(width)
    for c in range(C):
        product = dot(wb[...], nall[c].reshape(ff, cc))
        result = factor * (NEWTON_A * NEWTON_A * nall[c, r].astype(F32) + product)
        for b in range(F):
            tsend[c, b] = fold(result[b * q:(b + 1) * q]).astype(BF16)
        for k in range(1, F):
            t_copy(c, k).start()
        trecv[c][f] = tsend[c, f]

    for c in range(C):
        for k in range(1, F):
            t_arrival(c, k).wait_recv()
        for e in range(F):
            upd_ref[e, 0, :, cols(c)] = unfold(trecv[c][owners[e]].astype(F32)).astype(BF16)

    for c in range(C):
        for way in range(2):
            pos = position(way)
            for t in range(last):
                @pl.when(pos <= t)
                def _(c=c, way=way, t=t):
                    rs_copy(c, way, t).wait_send()

            @pl.when(pos < last)
            def _(c=c, way=way):
                own_copy(c, way).wait_send()

            for k in range(last - 1):
                @pl.when(jnp.logical_and(pos > k, pos < last))
                def _(c=c, way=way, k=k):
                    pass_copy(c, way, k).wait_send()
        for k in range(1, F):
            a_copy(c, k).wait_send()
            t_copy(c, k).wait_send()


def fused_step(grads, momentum, owner):
    Z, F = lax.axis_size("rep"), lax.axis_size("fsdp")
    q, width = momentum.shape[2], momentum.shape[3]
    C = CHUNKS
    cc = width // C
    rows = F * q
    ff = Z * rows
    vmem = pl.BlockSpec(memory_space=pltpu.VMEM)
    dma = pltpu.SemaphoreType.DMA
    return pl.pallas_call(
        functools.partial(step_kernel, Z, F, C),
        out_shape=(
            jax.ShapeDtypeStruct((F, 1, q, width), BF16),
            jax.ShapeDtypeStruct(momentum.shape, F32),
        ),
        in_specs=[pl.BlockSpec(memory_space=pltpu.SMEM), vmem, vmem],
        out_specs=(vmem, vmem),
        scratch_shapes=[
            pltpu.VMEM((Z, rows, width), F32),
            pltpu.VMEM((2, C, Z - 1, rows, cc), BF16),
            pltpu.VMEM((2, C, Z - 1, rows, cc), BF16),
            pltpu.VMEM((C, F, 2 * q, cc // 2), BF16),
            pltpu.VMEM((C, F, 2 * q, cc // 2), BF16),
            pltpu.VMEM((C, Z, rows, cc), BF16),
            pltpu.VMEM((ff, ff), F32),
            pltpu.VMEM((ff, ff), BF16),
            pltpu.VMEM((ff, ff), BF16),
            pltpu.VMEM((ff, ff), BF16),
            pltpu.VMEM((rows, ff), BF16),
            pltpu.VMEM((C, F, 2 * q, cc // 2), BF16),
            dma((2, C, Z - 1)),
            dma((2, C, Z - 1)),
            dma((C, F)),
            dma((C, F)),
            dma((2, C, Z - 1)),
            dma((2, C, Z - 1)),
            dma((C, F)),
            dma((C, F)),
        ] + [pltpu.VMEM((F, 2 * q, cc // 2), BF16)] * C,
        compiler_params=pltpu.CompilerParams(
            collective_id=0, has_side_effects=True, vmem_limit_bytes=58 * 1024 * 1024
        ),
        cost_estimate=pl.CostEstimate(
            flops=2 * ff * ff * width, bytes_accessed=16 * rows * width, transcendentals=0
        ),
    )(owner, grads, momentum)


def finish_rows(own_gram, gram_matrix):
    squared = jnp.dot(own_gram, gram_matrix, preferred_element_type=jnp.float32)
    polynomial = (NEWTON_B * own_gram.astype(jnp.float32) + NEWTON_C * squared).astype(jnp.bfloat16)
    return polynomial


def rows_whole(current, first_row):
    slab_rows = current.shape[0]
    result = current.astype(jnp.float32)
    for iteration in range(ITERS):
        gathered = lax.all_gather(current, "rep", axis=0, tiled=True)
        if iteration == 0:
            values = gathered.astype(jnp.float32)
            frobenius = jnp.sqrt(jnp.sum(values * values))
            whole = (values / (frobenius + EPSILON)).astype(jnp.bfloat16)
            mine = lax.dynamic_slice_in_dim(whole, first_row, slab_rows, 0)
        else:
            whole = gathered
            mine = current
        gram_matrix = lax.dot_general(
            whole, whole, (((1,), (1,)), ((), ())), preferred_element_type=jnp.float32
        ).astype(jnp.bfloat16)
        own_gram = lax.dynamic_slice_in_dim(gram_matrix, first_row, slab_rows, 0)
        polynomial = finish_rows(own_gram, gram_matrix)
        result = NEWTON_A * mine.astype(jnp.float32) + jnp.dot(
            polynomial, whole, preferred_element_type=jnp.float32
        )
        current = result.astype(jnp.bfloat16)
    return result


def on_device(grads, momentum, owner):
    slots = lax.axis_size("fsdp")
    replica = lax.axis_index("rep")
    width = grads.shape[-1]
    terms = grads[0].astype(jnp.float32)
    summed = lax.psum_scatter(terms, "rep", scatter_dimension=1, tiled=True)
    onehot = (owner[:, None] == jnp.arange(slots, dtype=jnp.int32)[None, :]).astype(jnp.float32)
    outgoing = jnp.einsum("es,eqd->sqd", onehot, summed, precision=lax.Precision.HIGHEST)
    arrived = lax.all_to_all(outgoing, "fsdp", split_axis=0, concat_axis=1, tiled=True)
    grad_rows = arrived[0]
    moment = momentum[0].reshape(-1, width)
    moment_new = DECAY_RATE * moment + grad_rows
    nesterov = (grad_rows + DECAY_RATE * moment_new).astype(jnp.bfloat16)
    slab_rows = nesterov.shape[0]
    first_row = replica * slab_rows
    result = rows_whole(nesterov, first_row)
    factor = math.sqrt(width)
    update_rows = (factor * result).astype(jnp.bfloat16)
    returning = lax.all_to_all(
        update_rows.reshape(slots, slab_rows // slots, width),
        "fsdp",
        split_axis=0,
        concat_axis=0,
        tiled=True,
    )
    updates = jnp.einsum(
        "es,sqd->eqd", onehot.astype(jnp.bfloat16), returning, preferred_element_type=jnp.float32
    ).astype(jnp.bfloat16)
    return (updates[:, None], moment_new.reshape(1, slots, slab_rows // slots, width))


def step(grads, momentum, owner):
    Z, F = lax.axis_size("rep"), lax.axis_size("fsdp")
    q, width = momentum.shape[2], momentum.shape[3]
    if q % 8 == 0 and F % 2 == 0 and Z % 2 == 0 and Z > 2 and width % (256 * CHUNKS) == 0:
        return fused_step(grads, momentum, owner)
    return on_device(grads, momentum, owner)


def solution(mesh):
    placed = (P("rep", None, "fsdp", None), P("fsdp", None, "rep", None), P())
    return jax.shard_map(
        step,
        mesh=mesh,
        in_specs=placed,
        out_specs=(P(None, "fsdp", "rep", None), P("fsdp", None, "rep", None)),
        check_vma=False,
    )
```

```python
import functools
import math

import jax
import jax.numpy as jnp
from jax import lax
from jax.experimental import pallas as pl
from jax.experimental.pallas import tpu as pltpu
from jax.sharding import PartitionSpec as P

ITERS = 2
CHUNKS = 8


DECAY_RATE = 0.95
NEWTON_A = 3.4445
NEWTON_B = -4.775
NEWTON_C = 2.0315
EPSILON = 1e-07
MESH = pl.DeviceIdType.MESH
F32 = jnp.float32
BF16 = jnp.bfloat16


def dot(left, right):
    return jnp.dot(left, right, preferred_element_type=F32)


def fold(block):
    half = block.shape[1] // 2
    return jnp.concatenate([block[:, :half], block[:, half:]], axis=0)


def unfold(block):
    half = block.shape[0] // 2
    return jnp.concatenate([block[:half], block[half:]], axis=1)


def schedule(Z, C):
    start, stride, exchange = 0.34, 0.8, 0.5
    stages = [(0.0, "prepare", 0)]
    stages += [(start + stride * t, "reduce", t) for t in range(Z - 1)]
    owner = start + stride * (Z - 1)
    stages += [(owner, "owner", 0), (owner + exchange, "momentum", 0)]
    stages += [(owner + exchange + stride * (k + 1), "gather", k) for k in range(Z - 1)]
    stages += [(owner + exchange + stride * (Z - 1) + 0.1, "gram", 0)]
    order = sorted((c + at, stage, c, n) for c in range(C) for at, stage, n in stages)
    return [item[1:] for item in order]


def step_kernel(
    Z, F, C,
    owner_ref, grads_hbm, mom_hbm,
    upd_ref, total_ref,
    g32, sbuf, rbuf, asend, arecv, nall, gacc, gb, pb, g2b, wb, tsend,
    rs_s, rs_r, a_s, a_r, ag_s, ag_r, t_s, t_r, mom_ref, load_sem, *split,
):
    trecv, loaded = split[:C], split[C:]
    r = lax.axis_index("rep")
    f = lax.axis_index("fsdp")
    q, width = mom_ref.shape[2], mom_ref.shape[3]
    cc = width // C
    rows = F * q
    ff = Z * rows
    last = Z - 1

    def load(c):
        return pltpu.make_async_copy(
            grads_hbm.at[0, :, :, pl.ds(c * cc, cc)], loaded[c], load_sem.at[c])

    mom_load = pltpu.make_async_copy(mom_hbm, mom_ref, load_sem.at[C])
    for c in range(C):
        load(c).start()
    mom_load.start()

    barrier = pltpu.get_barrier_semaphore()

    @pl.when(r > 0)
    def _():
        pl.semaphore_signal(barrier, inc=1, device_id={"rep": r - 1}, device_id_type=MESH)

    @pl.when(r < last)
    def _():
        pl.semaphore_signal(barrier, inc=1, device_id={"rep": r + 1}, device_id_type=MESH)

    for k in range(1, F):
        pl.semaphore_signal(barrier, inc=1, device_id={"fsdp": lax.rem(f + k, F)}, device_id_type=MESH)

    owners = [owner_ref[e] for e in range(F)]
    expert_of = []
    for s in range(F):
        found = jnp.int32(0)
        for e in range(1, F):
            found = jnp.where(owners[e] == s, jnp.int32(e), found)
        expert_of.append(found)

    def cols(c):
        return pl.ds(c * cc, cc)

    def prepare(c):
        load(c).wait()
        for s in range(F):
            block = loaded[c][expert_of[s]].astype(F32)
            for d in range(Z):
                g32[d, s * q:(s + 1) * q, cols(c)] = block[d * q:(d + 1) * q]

    def position(way):
        return r if way == 0 else last - r

    def ahead(way, n):
        return r + n if way == 0 else r - n

    def rs_copy(c, way, t):
        return pltpu.make_async_remote_copy(
            src_ref=sbuf.at[way, c, t], dst_ref=rbuf.at[way, c, t],
            send_sem=rs_s.at[way, c, t], recv_sem=rs_r.at[way, c, t],
            device_id={"rep": ahead(way, 1)}, device_id_type=MESH)

    def reduce_slot(c, t):
        for way in range(2):
            pos = position(way)
            dest = ahead(way, last - t)
            if t > 0:
                @pl.when(jnp.logical_and(pos > 0, pos <= t))
                def _(way=way, dest=dest):
                    rs_copy(c, way, t - 1).wait_recv()
                    sbuf[way, c, t] = (g32[dest, :, cols(c)] + rbuf[way, c, t - 1].astype(F32)).astype(BF16)
                    rs_copy(c, way, t).start()

            @pl.when(pos == 0)
            def _(way=way, dest=dest):
                sbuf[way, c, t] = g32[dest, :, cols(c)].astype(BF16)
                rs_copy(c, way, t).start()

    def a_copy(c, k):
        peer = lax.rem(f + k, F)
        return pltpu.make_async_remote_copy(
            src_ref=asend.at[c, peer], dst_ref=arecv.at[c, f],
            send_sem=a_s.at[c, k], recv_sem=a_r.at[c, k],
            device_id={"fsdp": peer}, device_id_type=MESH)

    def a_arrival(c, k):
        peer = lax.rem(f + F - k, F)
        return pltpu.make_async_remote_copy(
            src_ref=asend.at[c, peer], dst_ref=arecv.at[c, peer],
            send_sem=a_s.at[c, k], recv_sem=a_r.at[c, k],
            device_id={"fsdp": peer}, device_id_type=MESH)

    def reduce_last(c):
        for way in range(2):
            @pl.when(position(way) > 0)
            def _(way=way):
                rs_copy(c, way, last - 1).wait_recv()
                g32[r, :, cols(c)] += rbuf[way, c, last - 1].astype(F32)
        for s in range(F):
            asend[c, s] = fold(g32[r, s * q:(s + 1) * q, cols(c)]).astype(BF16)
        for k in range(1, F):
            a_copy(c, k).start()
        arecv[c, f] = asend[c, f]

    def own_copy(c, way):
        return pltpu.make_async_remote_copy(
            src_ref=nall.at[c, r], dst_ref=nall.at[c, r],
            send_sem=ag_s.at[way, c, 0], recv_sem=ag_r.at[way, c, 0],
            device_id={"rep": ahead(way, 1)}, device_id_type=MESH)

    def pass_copy(c, way, k):
        source = ahead(way, -1 - k)
        return pltpu.make_async_remote_copy(
            src_ref=nall.at[c, source], dst_ref=nall.at[c, source],
            send_sem=ag_s.at[way, c, k + 1], recv_sem=ag_r.at[way, c, k + 1],
            device_id={"rep": ahead(way, 1)}, device_id_type=MESH)

    def gather_arrival(c, way, k):
        source = ahead(way, -1 - k)
        return pltpu.make_async_remote_copy(
            src_ref=nall.at[c, source], dst_ref=nall.at[c, source],
            send_sem=ag_s.at[way, c, k], recv_sem=ag_r.at[way, c, k],
            device_id={"rep": ahead(way, -1)}, device_id_type=MESH)

    def momentum_rows(c):
        if c == 0:
            mom_load.wait()
        for k in range(1, F):
            a_arrival(c, k).wait_recv()
        for pair in range(F // 2):
            parts = []
            for b in (2 * pair, 2 * pair + 1):
                total = unfold(arecv[c, b].astype(F32))
                moved = DECAY_RATE * mom_ref[0, b, :, cols(c)] + total
                total_ref[0, b, :, cols(c)] = total.astype(BF16)
                parts.append(total + DECAY_RATE * moved)
            nall[c, r, 2 * pair * q:(2 * pair + 2) * q] = jnp.concatenate(parts, axis=0).astype(BF16)
        for way in range(2):
            @pl.when(position(way) < last)
            def _(way=way):
                own_copy(c, way).start()

    def gather_slot(c, k):
        for way in range(2):
            pos = position(way)

            @pl.when(pos > k)
            def _(way=way):
                gather_arrival(c, way, k).wait_recv()

            if k + 1 < last:
                @pl.when(jnp.logical_and(pos > k, pos < last))
                def _(way=way):
                    pass_copy(c, way, k).start()

    def row_blocks(body):
        size = ff // 2

        def step(i, carry):
            body(pl.ds(pl.multiple_of(i * size, size), size), i * size)
            return carry

        lax.fori_loop(0, 2, step, 0)

    def gram(c):
        if c % 2 == 1 and c < C - 1:
            return
        group = [c] if c in (0, C - 1) else [c - 1, c]
        half = Z // 2

        def step(i, carry):
            part = None
            for g in group:
                mine = nall[g, pl.ds(i * half, half)].reshape(half * rows, cc)
                term = lax.dot_general(
                    mine, nall[g].reshape(ff, cc), (((1,), (1,)), ((), ())), preferred_element_type=F32)
                part = term if part is None else part + term
            at = pl.ds(pl.multiple_of(i * half * rows, half * rows), half * rows)
            if c == 0:
                gacc[at, :] = part
            else:
                gacc[at, :] += part
            return carry

        lax.fori_loop(0, 2, step, 0)

    prepare(0)
    pl.semaphore_wait(barrier, (F - 1) + (r > 0).astype(jnp.int32) + (r < last).astype(jnp.int32))
    for stage, c, n in schedule(Z, C):
        if stage == "prepare" and c > 0:
            prepare(c)
        elif stage == "reduce":
            reduce_slot(c, n)
        elif stage == "owner":
            reduce_last(c)
        elif stage == "momentum":
            momentum_rows(c)
        elif stage == "gather":
            gather_slot(c, n)
        elif stage == "gram":
            gram(c)

    trace = jnp.zeros((1, 1), F32)
    size = ff // 2
    for i in range(2):
        at = slice(i * size, (i + 1) * size)
        row = lax.broadcasted_iota(jnp.int32, (size, size), 0)
        col = lax.broadcasted_iota(jnp.int32, (size, size), 1)
        trace += jnp.sum(jnp.where(row == col, gacc[at, at], 0.0), keepdims=True)
    scale = 1.0 / (jnp.sqrt(trace) + EPSILON)

    def normalise(at, _):
        scaled = gacc[at, :] * (scale * scale)
        gacc[at, :] = scaled
        gb[at, :] = scaled.astype(BF16)

    row_blocks(normalise)

    def first_polynomial(at, _):
        mine = gb[at, :]
        pb[at, :] = (NEWTON_B * mine.astype(F32) + NEWTON_C * dot(mine, gb[...])).astype(BF16)

    row_blocks(first_polynomial)

    def second_gram(at, _):
        mixed = dot(pb[at, :], gb[...])
        outer = dot(mixed.astype(BF16), pb[...])
        g2b[at, :] = (NEWTON_A * NEWTON_A * gacc[at, :] + 2.0 * NEWTON_A * mixed + outer).astype(BF16)

    row_blocks(second_gram)

    own = pl.ds(pl.multiple_of(r * rows, rows), rows)
    mine = g2b[own, :]
    second = (NEWTON_B * mine.astype(F32) + NEWTON_C * dot(mine, g2b[...])).astype(BF16)
    wb[...] = (
        NEWTON_A * (second.astype(F32) + pb[own, :].astype(F32)) + dot(second, pb[...])
    ).astype(BF16)

    def t_copy(c, k):
        peer = lax.rem(f + k, F)
        return pltpu.make_async_remote_copy(
            src_ref=tsend.at[c, peer], dst_ref=trecv[c].at[f],
            send_sem=t_s.at[c, k], recv_sem=t_r.at[c, k],
            device_id={"fsdp": peer}, device_id_type=MESH)

    def t_arrival(c, k):
        peer = lax.rem(f + F - k, F)
        return pltpu.make_async_remote_copy(
            src_ref=tsend.at[c, peer], dst_ref=trecv[c].at[peer],
            send_sem=t_s.at[c, k], recv_sem=t_r.at[c, k],
            device_id={"fsdp": peer}, device_id_type=MESH)

    factor = scale * math.sqrt(width)
    for c in range(C):
        product = dot(wb[...], nall[c].reshape(ff, cc))
        result = factor * (NEWTON_A * NEWTON_A * nall[c, r].astype(F32) + product)
        for b in range(F):
            tsend[c, b] = fold(result[b * q:(b + 1) * q]).astype(BF16)
        for k in range(1, F):
            t_copy(c, k).start()
        trecv[c][f] = tsend[c, f]

    for c in range(C):
        for k in range(1, F):
            t_arrival(c, k).wait_recv()
        for e in range(F):
            upd_ref[e, 0, :, cols(c)] = unfold(trecv[c][owners[e]].astype(F32)).astype(BF16)

    for c in range(C):
        for way in range(2):
            pos = position(way)
            for t in range(last):
                @pl.when(pos <= t)
                def _(c=c, way=way, t=t):
                    rs_copy(c, way, t).wait_send()

            @pl.when(pos < last)
            def _(c=c, way=way):
                own_copy(c, way).wait_send()

            for k in range(last - 1):
                @pl.when(jnp.logical_and(pos > k, pos < last))
                def _(c=c, way=way, k=k):
                    pass_copy(c, way, k).wait_send()
        for k in range(1, F):
            a_copy(c, k).wait_send()
            t_copy(c, k).wait_send()


def fused_step(grads, momentum, owner):
    Z, F = lax.axis_size("rep"), lax.axis_size("fsdp")
    q, width = momentum.shape[2], momentum.shape[3]
    C = CHUNKS
    cc = width // C
    rows = F * q
    ff = Z * rows
    vmem = pl.BlockSpec(memory_space=pltpu.VMEM)
    dma = pltpu.SemaphoreType.DMA
    any_place = pl.BlockSpec(memory_space=pl.ANY)
    updates, total = pl.pallas_call(
        functools.partial(step_kernel, Z, F, C),
        out_shape=(
            jax.ShapeDtypeStruct((F, 1, q, width), BF16),
            jax.ShapeDtypeStruct(momentum.shape, BF16),
        ),
        in_specs=[pl.BlockSpec(memory_space=pltpu.SMEM), any_place, any_place],
        out_specs=(vmem, vmem),
        scratch_shapes=[
            pltpu.VMEM((Z, rows, width), F32),
            pltpu.VMEM((2, C, Z - 1, rows, cc), BF16),
            pltpu.VMEM((2, C, Z - 1, rows, cc), BF16),
            pltpu.VMEM((C, F, 2 * q, cc // 2), BF16),
            pltpu.VMEM((C, F, 2 * q, cc // 2), BF16),
            pltpu.VMEM((C, Z, rows, cc), BF16),
            pltpu.VMEM((ff, ff), F32),
            pltpu.VMEM((ff, ff), BF16),
            pltpu.VMEM((ff, ff), BF16),
            pltpu.VMEM((ff, ff), BF16),
            pltpu.VMEM((rows, ff), BF16),
            pltpu.VMEM((C, F, 2 * q, cc // 2), BF16),
            dma((2, C, Z - 1)),
            dma((2, C, Z - 1)),
            dma((C, F)),
            dma((C, F)),
            dma((2, C, Z - 1)),
            dma((2, C, Z - 1)),
            dma((C, F)),
            dma((C, F)),
            pltpu.VMEM(momentum.shape, F32),
            dma((C + 1,)),
        ]
        + [pltpu.VMEM((F, 2 * q, cc // 2), BF16)] * C
        + [pltpu.VMEM(grads.shape[1:3] + (cc,), BF16)] * C,
        compiler_params=pltpu.CompilerParams(
            collective_id=0, has_side_effects=True, vmem_limit_bytes=58 * 1024 * 1024
        ),
        cost_estimate=pl.CostEstimate(
            flops=2 * ff * ff * width, bytes_accessed=16 * rows * width, transcendentals=0
        ),
    )(owner, grads, momentum)
    return updates, DECAY_RATE * momentum + total.astype(F32)


def finish_rows(own_gram, gram_matrix):
    squared = jnp.dot(own_gram, gram_matrix, preferred_element_type=jnp.float32)
    polynomial = (NEWTON_B * own_gram.astype(jnp.float32) + NEWTON_C * squared).astype(jnp.bfloat16)
    return polynomial


def rows_whole(current, first_row):
    slab_rows = current.shape[0]
    result = current.astype(jnp.float32)
    for iteration in range(ITERS):
        gathered = lax.all_gather(current, "rep", axis=0, tiled=True)
        if iteration == 0:
            values = gathered.astype(jnp.float32)
            frobenius = jnp.sqrt(jnp.sum(values * values))
            whole = (values / (frobenius + EPSILON)).astype(jnp.bfloat16)
            mine = lax.dynamic_slice_in_dim(whole, first_row, slab_rows, 0)
        else:
            whole = gathered
            mine = current
        gram_matrix = lax.dot_general(
            whole, whole, (((1,), (1,)), ((), ())), preferred_element_type=jnp.float32
        ).astype(jnp.bfloat16)
        own_gram = lax.dynamic_slice_in_dim(gram_matrix, first_row, slab_rows, 0)
        polynomial = finish_rows(own_gram, gram_matrix)
        result = NEWTON_A * mine.astype(jnp.float32) + jnp.dot(
            polynomial, whole, preferred_element_type=jnp.float32
        )
        current = result.astype(jnp.bfloat16)
    return result


def on_device(grads, momentum, owner):
    slots = lax.axis_size("fsdp")
    replica = lax.axis_index("rep")
    width = grads.shape[-1]
    terms = grads[0].astype(jnp.float32)
    summed = lax.psum_scatter(terms, "rep", scatter_dimension=1, tiled=True)
    onehot = (owner[:, None] == jnp.arange(slots, dtype=jnp.int32)[None, :]).astype(jnp.float32)
    outgoing = jnp.einsum("es,eqd->sqd", onehot, summed, precision=lax.Precision.HIGHEST)
    arrived = lax.all_to_all(outgoing, "fsdp", split_axis=0, concat_axis=1, tiled=True)
    grad_rows = arrived[0]
    moment = momentum[0].reshape(-1, width)
    moment_new = DECAY_RATE * moment + grad_rows
    nesterov = (grad_rows + DECAY_RATE * moment_new).astype(jnp.bfloat16)
    slab_rows = nesterov.shape[0]
    first_row = replica * slab_rows
    result = rows_whole(nesterov, first_row)
    factor = math.sqrt(width)
    update_rows = (factor * result).astype(jnp.bfloat16)
    returning = lax.all_to_all(
        update_rows.reshape(slots, slab_rows // slots, width),
        "fsdp",
        split_axis=0,
        concat_axis=0,
        tiled=True,
    )
    updates = jnp.einsum(
        "es,sqd->eqd", onehot.astype(jnp.bfloat16), returning, preferred_element_type=jnp.float32
    ).astype(jnp.bfloat16)
    return (updates[:, None], moment_new.reshape(1, slots, slab_rows // slots, width))


def step(grads, momentum, owner):
    Z, F = lax.axis_size("rep"), lax.axis_size("fsdp")
    q, width = momentum.shape[2], momentum.shape[3]
    if q % 8 == 0 and F % 2 == 0 and Z % 2 == 0 and Z > 2 and width % (256 * CHUNKS) == 0:
        return fused_step(grads, momentum, owner)
    return on_device(grads, momentum, owner)


def solution(mesh):
    placed = (P("rep", None, "fsdp", None), P("fsdp", None, "rep", None), P())
    return jax.shard_map(
        step,
        mesh=mesh,
        in_specs=placed,
        out_specs=(P(None, "fsdp", "rep", None), P("fsdp", None, "rep", None)),
        check_vma=False,
    )
```

```python
import functools
import math

import jax
import jax.numpy as jnp
from jax import lax
from jax.experimental import pallas as pl
from jax.experimental.pallas import tpu as pltpu
from jax.sharding import PartitionSpec as P

ITERS = 2
CHUNKS = 8


DECAY_RATE = 0.95
NEWTON_A = 3.4445
NEWTON_B = -4.775
NEWTON_C = 2.0315
EPSILON = 1e-07
MESH = pl.DeviceIdType.MESH
F32 = jnp.float32
BF16 = jnp.bfloat16


def dot(left, right):
    return jnp.dot(left, right, preferred_element_type=F32)


def fold(block):
    half = block.shape[1] // 2
    return jnp.concatenate([block[:, :half], block[:, half:]], axis=0)


def unfold(block):
    half = block.shape[0] // 2
    return jnp.concatenate([block[:half], block[half:]], axis=1)


def schedule(Z, C):
    start, stride, exchange = 0.34, 0.8, 0.5
    stages = [(0.0, "prepare", 0)]
    stages += [(start + stride * t, "reduce", t) for t in range(Z - 1)]
    owner = start + stride * (Z - 1)
    stages += [(owner, "owner", 0), (owner + exchange, "momentum", 0)]
    stages += [(owner + exchange + stride * (k + 1), "gather", k) for k in range(Z - 1)]
    stages += [(owner + exchange + stride * (Z - 1) + 0.1, "gram", 0)]
    order = sorted((c + at, stage, c, n) for c in range(C) for at, stage, n in stages)
    return [item[1:] for item in order]


def step_kernel(
    Z, F, C,
    owner_ref, grads_hbm, mom_hbm,
    upd_ref, total_ref,
    g32, sbuf, rbuf, asend, arecv, nall, gacc, gb, pb, g2b, wb, tsend,
    rs_s, rs_r, a_s, a_r, ag_s, ag_r, t_s, t_r, mom_ref, load_sem, *split,
):
    trecv, loaded = split[:C // 2], split[C // 2:]
    r = lax.axis_index("rep")
    f = lax.axis_index("fsdp")
    q, width = mom_ref.shape[2], mom_ref.shape[3]
    cc = width // C
    rows = F * q
    ff = Z * rows
    last = Z - 1

    def load(c):
        return pltpu.make_async_copy(
            grads_hbm.at[0, :, :, pl.ds(c * cc, cc)], loaded[c], load_sem.at[c])

    mom_load = pltpu.make_async_copy(mom_hbm, mom_ref, load_sem.at[C])
    for c in range(C):
        load(c).start()
    mom_load.start()

    barrier = pltpu.get_barrier_semaphore()

    @pl.when(r > 0)
    def _():
        pl.semaphore_signal(barrier, inc=1, device_id={"rep": r - 1}, device_id_type=MESH)

    @pl.when(r < last)
    def _():
        pl.semaphore_signal(barrier, inc=1, device_id={"rep": r + 1}, device_id_type=MESH)

    for k in range(1, F):
        pl.semaphore_signal(barrier, inc=1, device_id={"fsdp": lax.rem(f + k, F)}, device_id_type=MESH)

    owners = [owner_ref[e] for e in range(F)]
    expert_of = []
    for s in range(F):
        found = jnp.int32(0)
        for e in range(1, F):
            found = jnp.where(owners[e] == s, jnp.int32(e), found)
        expert_of.append(found)

    def cols(c):
        return pl.ds(c * cc, cc)

    def prepare(c):
        load(c).wait()
        for s in range(F):
            block = loaded[c][expert_of[s]].astype(F32)
            for d in range(Z):
                g32[d, s * q:(s + 1) * q, cols(c)] = block[d * q:(d + 1) * q]

    def position(way):
        return r if way == 0 else last - r

    def ahead(way, n):
        return r + n if way == 0 else r - n

    def rs_copy(c, way, t):
        return pltpu.make_async_remote_copy(
            src_ref=sbuf.at[way, c, t], dst_ref=rbuf.at[way, c, t],
            send_sem=rs_s.at[way, c, t], recv_sem=rs_r.at[way, c, t],
            device_id={"rep": ahead(way, 1)}, device_id_type=MESH)

    def reduce_slot(c, t):
        for way in range(2):
            pos = position(way)
            dest = ahead(way, last - t)
            if t > 0:
                @pl.when(jnp.logical_and(pos > 0, pos <= t))
                def _(way=way, dest=dest):
                    rs_copy(c, way, t - 1).wait_recv()
                    sbuf[way, c, t] = (g32[dest, :, cols(c)] + rbuf[way, c, t - 1].astype(F32)).astype(BF16)
                    rs_copy(c, way, t).start()

            @pl.when(pos == 0)
            def _(way=way, dest=dest):
                sbuf[way, c, t] = g32[dest, :, cols(c)].astype(BF16)
                rs_copy(c, way, t).start()

    def a_copy(c, k):
        peer = lax.rem(f + k, F)
        return pltpu.make_async_remote_copy(
            src_ref=asend.at[c, peer], dst_ref=arecv.at[c, f],
            send_sem=a_s.at[c, k], recv_sem=a_r.at[c, k],
            device_id={"fsdp": peer}, device_id_type=MESH)

    def a_arrival(c, k):
        peer = lax.rem(f + F - k, F)
        return pltpu.make_async_remote_copy(
            src_ref=asend.at[c, peer], dst_ref=arecv.at[c, peer],
            send_sem=a_s.at[c, k], recv_sem=a_r.at[c, k],
            device_id={"fsdp": peer}, device_id_type=MESH)

    def reduce_last(c):
        for way in range(2):
            @pl.when(position(way) > 0)
            def _(way=way):
                rs_copy(c, way, last - 1).wait_recv()
                g32[r, :, cols(c)] += rbuf[way, c, last - 1].astype(F32)
        for k in range(1, F):
            peer = lax.rem(f + k, F)
            asend[c, peer] = fold(g32[r, pl.ds(pl.multiple_of(peer * q, q), q), cols(c)]).astype(BF16)
            a_copy(c, k).start()
        arecv[c, f] = fold(g32[r, pl.ds(pl.multiple_of(f * q, q), q), cols(c)]).astype(BF16)

    def own_copy(c, way):
        return pltpu.make_async_remote_copy(
            src_ref=nall.at[c, r], dst_ref=nall.at[c, r],
            send_sem=ag_s.at[way, c, 0], recv_sem=ag_r.at[way, c, 0],
            device_id={"rep": ahead(way, 1)}, device_id_type=MESH)

    def pass_copy(c, way, k):
        source = ahead(way, -1 - k)
        return pltpu.make_async_remote_copy(
            src_ref=nall.at[c, source], dst_ref=nall.at[c, source],
            send_sem=ag_s.at[way, c, k + 1], recv_sem=ag_r.at[way, c, k + 1],
            device_id={"rep": ahead(way, 1)}, device_id_type=MESH)

    def gather_arrival(c, way, k):
        source = ahead(way, -1 - k)
        return pltpu.make_async_remote_copy(
            src_ref=nall.at[c, source], dst_ref=nall.at[c, source],
            send_sem=ag_s.at[way, c, k], recv_sem=ag_r.at[way, c, k],
            device_id={"rep": ahead(way, -1)}, device_id_type=MESH)

    def momentum_rows(c):
        if c == 0:
            mom_load.wait()
        for k in range(1, F):
            a_arrival(c, k).wait_recv()
        for pair in range(F // 2):
            parts = []
            for b in (2 * pair, 2 * pair + 1):
                total = unfold(arecv[c, b].astype(F32))
                moved = DECAY_RATE * mom_ref[0, b, :, cols(c)] + total
                total_ref[0, b, :, cols(c)] = total.astype(BF16)
                parts.append(total + DECAY_RATE * moved)
            nall[c, r, 2 * pair * q:(2 * pair + 2) * q] = jnp.concatenate(parts, axis=0).astype(BF16)
        for way in range(2):
            @pl.when(position(way) < last)
            def _(way=way):
                own_copy(c, way).start()

    def gather_slot(c, k):
        for way in range(2):
            pos = position(way)

            @pl.when(pos > k)
            def _(way=way):
                gather_arrival(c, way, k).wait_recv()

            if k + 1 < last:
                @pl.when(jnp.logical_and(pos > k, pos < last))
                def _(way=way):
                    pass_copy(c, way, k).start()

    def row_blocks(body):
        size = ff // 2

        def step(i, carry):
            body(pl.ds(pl.multiple_of(i * size, size), size), i * size)
            return carry

        lax.fori_loop(0, 2, step, 0)

    def gram(c):
        if c % 2 == 1 and c < C - 1:
            return
        group = [c] if c in (0, C - 1) else [c - 1, c]
        half = Z // 2

        def step(i, carry):
            part = None
            for g in group:
                mine = nall[g, pl.ds(i * half, half)].reshape(half * rows, cc)
                term = lax.dot_general(
                    mine, nall[g].reshape(ff, cc), (((1,), (1,)), ((), ())), preferred_element_type=F32)
                part = term if part is None else part + term
            at = pl.ds(pl.multiple_of(i * half * rows, half * rows), half * rows)
            if c == 0:
                gacc[at, :] = part
            else:
                gacc[at, :] += part
            return carry

        lax.fori_loop(0, 2, step, 0)

    prepare(0)
    pl.semaphore_wait(barrier, (F - 1) + (r > 0).astype(jnp.int32) + (r < last).astype(jnp.int32))
    for stage, c, n in schedule(Z, C):
        if stage == "prepare" and c > 0:
            prepare(c)
        elif stage == "reduce":
            reduce_slot(c, n)
        elif stage == "owner":
            reduce_last(c)
        elif stage == "momentum":
            momentum_rows(c)
        elif stage == "gather":
            gather_slot(c, n)
        elif stage == "gram":
            gram(c)

    trace = jnp.zeros((1, 1), F32)
    size = ff // 2
    for i in range(2):
        at = slice(i * size, (i + 1) * size)
        row = lax.broadcasted_iota(jnp.int32, (size, size), 0)
        col = lax.broadcasted_iota(jnp.int32, (size, size), 1)
        trace += jnp.sum(jnp.where(row == col, gacc[at, at], 0.0), keepdims=True)
    scale = 1.0 / (jnp.sqrt(trace) + EPSILON)

    def normalise(at, _):
        gb[at, :] = (gacc[at, :] * (scale * scale)).astype(BF16)

    row_blocks(normalise)

    def first_polynomial(at, _):
        mine = gb[at, :]
        pb[at, :] = (NEWTON_B * mine.astype(F32) + NEWTON_C * dot(mine, gb[...])).astype(BF16)

    row_blocks(first_polynomial)

    def second_gram(at, _):
        mixed = dot(pb[at, :], gb[...])
        outer = dot(mixed.astype(BF16), pb[...])
        g2b[at, :] = (NEWTON_A * NEWTON_A * (gacc[at, :] * (scale * scale)) + 2.0 * NEWTON_A * mixed + outer).astype(BF16)

    row_blocks(second_gram)

    own = pl.ds(pl.multiple_of(r * rows, rows), rows)
    mine = g2b[own, :]
    second = (NEWTON_B * mine.astype(F32) + NEWTON_C * dot(mine, g2b[...])).astype(BF16)
    wb[...] = (
        NEWTON_A * (second.astype(F32) + pb[own, :].astype(F32)) + dot(second, pb[...])
    ).astype(BF16)

    def t_copy(c, k):
        peer = lax.rem(f + k, F)
        return pltpu.make_async_remote_copy(
            src_ref=tsend.at[c, peer], dst_ref=trecv[c].at[f],
            send_sem=t_s.at[c, k], recv_sem=t_r.at[c, k],
            device_id={"fsdp": peer}, device_id_type=MESH)

    def t_arrival(c, k):
        peer = lax.rem(f + F - k, F)
        return pltpu.make_async_remote_copy(
            src_ref=tsend.at[c, peer], dst_ref=trecv[c].at[peer],
            send_sem=t_s.at[c, k], recv_sem=t_r.at[c, k],
            device_id={"fsdp": peer}, device_id_type=MESH)

    factor = scale * math.sqrt(width)
    for g in range(C // 2):
        halves = []
        for c in (2 * g, 2 * g + 1):
            product = dot(wb[...], nall[c].reshape(ff, cc))
            halves.append(factor * (NEWTON_A * NEWTON_A * nall[c, r].astype(F32) + product))
        for b in range(F):
            tsend[g, b] = jnp.concatenate([half[b * q:(b + 1) * q] for half in halves], axis=0).astype(BF16)
        for k in range(1, F):
            t_copy(g, k).start()
        trecv[g][f] = tsend[g, f]

    for g in range(C // 2):
        for k in range(1, F):
            t_arrival(g, k).wait_recv()
        for e in range(F):
            upd_ref[e, 0, :, pl.ds(2 * g * cc, 2 * cc)] = unfold(trecv[g][owners[e]].astype(F32)).astype(BF16)

    for c in range(C):
        for way in range(2):
            pos = position(way)
            for t in range(last):
                @pl.when(pos <= t)
                def _(c=c, way=way, t=t):
                    rs_copy(c, way, t).wait_send()

            @pl.when(pos < last)
            def _(c=c, way=way):
                own_copy(c, way).wait_send()

            for k in range(last - 1):
                @pl.when(jnp.logical_and(pos > k, pos < last))
                def _(c=c, way=way, k=k):
                    pass_copy(c, way, k).wait_send()
        for k in range(1, F):
            a_copy(c, k).wait_send()
    for g in range(C // 2):
        for k in range(1, F):
            t_copy(g, k).wait_send()


def fused_step(grads, momentum, owner):
    Z, F = lax.axis_size("rep"), lax.axis_size("fsdp")
    q, width = momentum.shape[2], momentum.shape[3]
    C = CHUNKS
    cc = width // C
    rows = F * q
    ff = Z * rows
    vmem = pl.BlockSpec(memory_space=pltpu.VMEM)
    dma = pltpu.SemaphoreType.DMA
    any_place = pl.BlockSpec(memory_space=pl.ANY)
    updates, total = pl.pallas_call(
        functools.partial(step_kernel, Z, F, C),
        out_shape=(
            jax.ShapeDtypeStruct((F, 1, q, width), BF16),
            jax.ShapeDtypeStruct(momentum.shape, BF16),
        ),
        in_specs=[pl.BlockSpec(memory_space=pltpu.SMEM), any_place, any_place],
        out_specs=(vmem, vmem),
        scratch_shapes=[
            pltpu.VMEM((Z, rows, width), F32),
            pltpu.VMEM((2, C, Z - 1, rows, cc), BF16),
            pltpu.VMEM((2, C, Z - 1, rows, cc), BF16),
            pltpu.VMEM((C, F, 2 * q, cc // 2), BF16),
            pltpu.VMEM((C, F, 2 * q, cc // 2), BF16),
            pltpu.VMEM((C, Z, rows, cc), BF16),
            pltpu.VMEM((ff, ff), F32),
            pltpu.VMEM((ff, ff), BF16),
            pltpu.VMEM((ff, ff), BF16),
            pltpu.VMEM((ff, ff), BF16),
            pltpu.VMEM((rows, ff), BF16),
            pltpu.VMEM((C // 2, F, 2 * q, cc), BF16),
            dma((2, C, Z - 1)),
            dma((2, C, Z - 1)),
            dma((C, F)),
            dma((C, F)),
            dma((2, C, Z - 1)),
            dma((2, C, Z - 1)),
            dma((C, F)),
            dma((C, F)),
            pltpu.VMEM(momentum.shape, F32),
            dma((C + 1,)),
        ]
        + [pltpu.VMEM((F, 2 * q, cc), BF16)] * (C // 2)
        + [pltpu.VMEM(grads.shape[1:3] + (cc,), BF16)] * C,
        compiler_params=pltpu.CompilerParams(
            collective_id=0, has_side_effects=True, vmem_limit_bytes=58 * 1024 * 1024
        ),
        cost_estimate=pl.CostEstimate(
            flops=2 * ff * ff * width, bytes_accessed=16 * rows * width, transcendentals=0
        ),
    )(owner, grads, momentum)
    return updates, DECAY_RATE * momentum + total.astype(F32)


def finish_rows(own_gram, gram_matrix):
    squared = jnp.dot(own_gram, gram_matrix, preferred_element_type=jnp.float32)
    polynomial = (NEWTON_B * own_gram.astype(jnp.float32) + NEWTON_C * squared).astype(jnp.bfloat16)
    return polynomial


def rows_whole(current, first_row):
    slab_rows = current.shape[0]
    result = current.astype(jnp.float32)
    for iteration in range(ITERS):
        gathered = lax.all_gather(current, "rep", axis=0, tiled=True)
        if iteration == 0:
            values = gathered.astype(jnp.float32)
            frobenius = jnp.sqrt(jnp.sum(values * values))
            whole = (values / (frobenius + EPSILON)).astype(jnp.bfloat16)
            mine = lax.dynamic_slice_in_dim(whole, first_row, slab_rows, 0)
        else:
            whole = gathered
            mine = current
        gram_matrix = lax.dot_general(
            whole, whole, (((1,), (1,)), ((), ())), preferred_element_type=jnp.float32
        ).astype(jnp.bfloat16)
        own_gram = lax.dynamic_slice_in_dim(gram_matrix, first_row, slab_rows, 0)
        polynomial = finish_rows(own_gram, gram_matrix)
        result = NEWTON_A * mine.astype(jnp.float32) + jnp.dot(
            polynomial, whole, preferred_element_type=jnp.float32
        )
        current = result.astype(jnp.bfloat16)
    return result


def on_device(grads, momentum, owner):
    slots = lax.axis_size("fsdp")
    replica = lax.axis_index("rep")
    width = grads.shape[-1]
    terms = grads[0].astype(jnp.float32)
    summed = lax.psum_scatter(terms, "rep", scatter_dimension=1, tiled=True)
    onehot = (owner[:, None] == jnp.arange(slots, dtype=jnp.int32)[None, :]).astype(jnp.float32)
    outgoing = jnp.einsum("es,eqd->sqd", onehot, summed, precision=lax.Precision.HIGHEST)
    arrived = lax.all_to_all(outgoing, "fsdp", split_axis=0, concat_axis=1, tiled=True)
    grad_rows = arrived[0]
    moment = momentum[0].reshape(-1, width)
    moment_new = DECAY_RATE * moment + grad_rows
    nesterov = (grad_rows + DECAY_RATE * moment_new).astype(jnp.bfloat16)
    slab_rows = nesterov.shape[0]
    first_row = replica * slab_rows
    result = rows_whole(nesterov, first_row)
    factor = math.sqrt(width)
    update_rows = (factor * result).astype(jnp.bfloat16)
    returning = lax.all_to_all(
        update_rows.reshape(slots, slab_rows // slots, width),
        "fsdp",
        split_axis=0,
        concat_axis=0,
        tiled=True,
    )
    updates = jnp.einsum(
        "es,sqd->eqd", onehot.astype(jnp.bfloat16), returning, preferred_element_type=jnp.float32
    ).astype(jnp.bfloat16)
    return (updates[:, None], moment_new.reshape(1, slots, slab_rows // slots, width))


def step(grads, momentum, owner):
    Z, F = lax.axis_size("rep"), lax.axis_size("fsdp")
    q, width = momentum.shape[2], momentum.shape[3]
    if q % 8 == 0 and F % 2 == 0 and Z % 2 == 0 and Z > 2 and width % (256 * CHUNKS) == 0:
        return fused_step(grads, momentum, owner)
    return on_device(grads, momentum, owner)


def solution(mesh):
    placed = (P("rep", None, "fsdp", None), P("fsdp", None, "rep", None), P())
    return jax.shard_map(
        step,
        mesh=mesh,
        in_specs=placed,
        out_specs=(P(None, "fsdp", "rep", None), P("fsdp", None, "rep", None)),
        check_vma=False,
    )
```

```python
import functools
import math

import jax
import jax.numpy as jnp
from jax import lax
from jax.experimental import pallas as pl
from jax.experimental.pallas import tpu as pltpu
from jax.sharding import PartitionSpec as P

ITERS = 2
CHUNKS = 8


DECAY_RATE = 0.95
NEWTON_A = 3.4445
NEWTON_B = -4.775
NEWTON_C = 2.0315
EPSILON = 1e-07
MESH = pl.DeviceIdType.MESH
F32 = jnp.float32
BF16 = jnp.bfloat16


def dot(left, right):
    return jnp.dot(left, right, preferred_element_type=F32)


def fold(block):
    half = block.shape[1] // 2
    return jnp.concatenate([block[:, :half], block[:, half:]], axis=0)


def unfold(block):
    half = block.shape[0] // 2
    return jnp.concatenate([block[:half], block[half:]], axis=1)


def schedule(Z, C):
    start, stride, exchange = 0.34, 0.8, 0.5
    stages = [(0.0, "prepare", 0)]
    stages += [(start + stride * t, "reduce", t) for t in range(Z - 1)]
    owner = start + stride * (Z - 1)
    stages += [(owner, "owner", 0), (owner + exchange, "momentum", 0)]
    stages += [(owner + exchange + stride * (k + 1), "gather", k) for k in range(Z - 1)]
    stages += [(owner + exchange + stride * (Z - 1) + 0.33, "gram", 0)]
    order = sorted((c + at, stage, c, n) for c in range(C) for at, stage, n in stages)
    return [item[1:] for item in order]


def step_kernel(
    Z, F, C,
    owner_ref, grads_hbm, mom_hbm,
    upd_ref, total_ref,
    g32, sbuf, rbuf, asend, arecv, nall, gacc, gb, pb, g2b, wb, tsend,
    rs_s, rs_r, a_s, a_r, ag_s, ag_r, t_s, t_r, mom_ref, load_sem, *split,
):
    trecv, loaded = split[:C], split[C:]
    r = lax.axis_index("rep")
    f = lax.axis_index("fsdp")
    q, width = mom_ref.shape[2], mom_ref.shape[3]
    cc = width // C
    rows = F * q
    ff = Z * rows
    last = Z - 1

    def load(c):
        return pltpu.make_async_copy(
            grads_hbm.at[0, :, :, pl.ds(c * cc, cc)], loaded[c], load_sem.at[c])

    mom_load = pltpu.make_async_copy(mom_hbm, mom_ref, load_sem.at[C])
    for c in range(C):
        load(c).start()
    mom_load.start()

    barrier = pltpu.get_barrier_semaphore()

    @pl.when(r > 0)
    def _():
        pl.semaphore_signal(barrier, inc=1, device_id={"rep": r - 1}, device_id_type=MESH)

    @pl.when(r < last)
    def _():
        pl.semaphore_signal(barrier, inc=1, device_id={"rep": r + 1}, device_id_type=MESH)

    for k in range(1, F):
        pl.semaphore_signal(barrier, inc=1, device_id={"fsdp": lax.rem(f + k, F)}, device_id_type=MESH)

    owners = [owner_ref[e] for e in range(F)]
    expert_of = []
    for s in range(F):
        found = jnp.int32(0)
        for e in range(1, F):
            found = jnp.where(owners[e] == s, jnp.int32(e), found)
        expert_of.append(found)

    def cols(c):
        return pl.ds(c * cc, cc)

    def prepare(c):
        load(c).wait()
        for s in range(F):
            block = loaded[c][expert_of[s]].astype(F32)
            for d in range(Z):
                g32[d, s * q:(s + 1) * q, cols(c)] = block[d * q:(d + 1) * q]

    def position(way):
        return r if way == 0 else last - r

    def ahead(way, n):
        return r + n if way == 0 else r - n

    def rs_copy(c, way, t):
        return pltpu.make_async_remote_copy(
            src_ref=sbuf.at[way, c, t], dst_ref=rbuf.at[way, c, t],
            send_sem=rs_s.at[way, c, t], recv_sem=rs_r.at[way, c, t],
            device_id={"rep": ahead(way, 1)}, device_id_type=MESH)

    def reduce_slot(c, t):
        for way in range(2):
            pos = position(way)
            dest = ahead(way, last - t)
            if t > 0:
                @pl.when(jnp.logical_and(pos > 0, pos <= t))
                def _(way=way, dest=dest):
                    rs_copy(c, way, t - 1).wait_recv()
                    sbuf[way, c, t] = (g32[dest, :, cols(c)] + rbuf[way, c, t - 1].astype(F32)).astype(BF16)
                    rs_copy(c, way, t).start()

            @pl.when(pos == 0)
            def _(way=way, dest=dest):
                sbuf[way, c, t] = g32[dest, :, cols(c)].astype(BF16)
                rs_copy(c, way, t).start()

    def a_copy(c, k):
        peer = lax.rem(f + k, F)
        return pltpu.make_async_remote_copy(
            src_ref=asend.at[c, peer], dst_ref=arecv.at[c, f],
            send_sem=a_s.at[c, k], recv_sem=a_r.at[c, k],
            device_id={"fsdp": peer}, device_id_type=MESH)

    def a_arrival(c, k):
        peer = lax.rem(f + F - k, F)
        return pltpu.make_async_remote_copy(
            src_ref=asend.at[c, peer], dst_ref=arecv.at[c, peer],
            send_sem=a_s.at[c, k], recv_sem=a_r.at[c, k],
            device_id={"fsdp": peer}, device_id_type=MESH)

    def reduce_last(c):
        for way in range(2):
            @pl.when(position(way) > 0)
            def _(way=way):
                rs_copy(c, way, last - 1).wait_recv()
                g32[r, :, cols(c)] += rbuf[way, c, last - 1].astype(F32)
        for s in range(F):
            asend[c, s] = fold(g32[r, s * q:(s + 1) * q, cols(c)]).astype(BF16)
        for k in range(1, F):
            a_copy(c, k).start()
        arecv[c, f] = asend[c, f]

    def own_copy(c, way):
        return pltpu.make_async_remote_copy(
            src_ref=nall.at[c, r], dst_ref=nall.at[c, r],
            send_sem=ag_s.at[way, c, 0], recv_sem=ag_r.at[way, c, 0],
            device_id={"rep": ahead(way, 1)}, device_id_type=MESH)

    def pass_copy(c, way, k):
        source = ahead(way, -1 - k)
        return pltpu.make_async_remote_copy(
            src_ref=nall.at[c, source], dst_ref=nall.at[c, source],
            send_sem=ag_s.at[way, c, k + 1], recv_sem=ag_r.at[way, c, k + 1],
            device_id={"rep": ahead(way, 1)}, device_id_type=MESH)

    def gather_arrival(c, way, k):
        source = ahead(way, -1 - k)
        return pltpu.make_async_remote_copy(
            src_ref=nall.at[c, source], dst_ref=nall.at[c, source],
            send_sem=ag_s.at[way, c, k], recv_sem=ag_r.at[way, c, k],
            device_id={"rep": ahead(way, -1)}, device_id_type=MESH)

    def momentum_rows(c):
        if c == 0:
            mom_load.wait()
        for k in range(1, F):
            a_arrival(c, k).wait_recv()
        for pair in range(F // 2):
            parts = []
            for b in (2 * pair, 2 * pair + 1):
                total = unfold(arecv[c, b].astype(F32))
                moved = DECAY_RATE * mom_ref[0, b, :, cols(c)] + total
                total_ref[0, b, :, cols(c)] = total.astype(BF16)
                parts.append(total + DECAY_RATE * moved)
            nall[c, r, 2 * pair * q:(2 * pair + 2) * q] = jnp.concatenate(parts, axis=0).astype(BF16)
        for way in range(2):
            @pl.when(position(way) < last)
            def _(way=way):
                own_copy(c, way).start()

    def gather_slot(c, k):
        for way in range(2):
            pos = position(way)

            @pl.when(pos > k)
            def _(way=way):
                gather_arrival(c, way, k).wait_recv()

            if k + 1 < last:
                @pl.when(jnp.logical_and(pos > k, pos < last))
                def _(way=way):
                    pass_copy(c, way, k).start()

    def row_blocks(body):
        size = ff // 2

        def step(i, carry):
            body(pl.ds(pl.multiple_of(i * size, size), size), i * size)
            return carry

        lax.fori_loop(0, 2, step, 0)

    def gram(c):
        if c % 2 == 1 and c < C - 1:
            return
        group = [c] if c in (0, C - 1) else [c - 1, c]
        half = Z // 2

        def step(i, carry):
            part = None
            for g in group:
                mine = nall[g, pl.ds(i * half, half)].reshape(half * rows, cc)
                term = lax.dot_general(
                    mine, nall[g].reshape(ff, cc), (((1,), (1,)), ((), ())), preferred_element_type=F32)
                part = term if part is None else part + term
            at = pl.ds(pl.multiple_of(i * half * rows, half * rows), half * rows)
            if c == 0:
                gacc[at, :] = part
            else:
                gacc[at, :] += part
            return carry

        lax.fori_loop(0, 2, step, 0)

    prepare(0)
    pl.semaphore_wait(barrier, (F - 1) + (r > 0).astype(jnp.int32) + (r < last).astype(jnp.int32))
    for stage, c, n in schedule(Z, C):
        if stage == "prepare" and c > 0:
            prepare(c)
        elif stage == "reduce":
            reduce_slot(c, n)
        elif stage == "owner":
            reduce_last(c)
        elif stage == "momentum":
            momentum_rows(c)
        elif stage == "gather":
            gather_slot(c, n)
        elif stage == "gram":
            gram(c)

    trace = jnp.zeros((1, 1), F32)
    size = ff // 2
    for i in range(2):
        at = slice(i * size, (i + 1) * size)
        row = lax.broadcasted_iota(jnp.int32, (size, size), 0)
        col = lax.broadcasted_iota(jnp.int32, (size, size), 1)
        trace += jnp.sum(jnp.where(row == col, gacc[at, at], 0.0), keepdims=True)
    scale = 1.0 / (jnp.sqrt(trace) + EPSILON)

    def normalise(at, _):
        scaled = gacc[at, :] * (scale * scale)
        gacc[at, :] = scaled
        gb[at, :] = scaled.astype(BF16)

    row_blocks(normalise)

    def first_polynomial(at, _):
        mine = gb[at, :]
        pb[at, :] = (NEWTON_B * mine.astype(F32) + NEWTON_C * dot(mine, gb[...])).astype(BF16)

    row_blocks(first_polynomial)

    def second_gram(at, _):
        mixed = dot(pb[at, :], gb[...])
        outer = dot(mixed.astype(BF16), pb[...])
        g2b[at, :] = (NEWTON_A * NEWTON_A * gacc[at, :] + 2.0 * NEWTON_A * mixed + outer).astype(BF16)

    row_blocks(second_gram)

    own = pl.ds(pl.multiple_of(r * rows, rows), rows)
    mine = g2b[own, :]
    second = (NEWTON_B * mine.astype(F32) + NEWTON_C * dot(mine, g2b[...])).astype(BF16)
    wb[...] = (
        NEWTON_A * (second.astype(F32) + pb[own, :].astype(F32)) + dot(second, pb[...])
    ).astype(BF16)

    def t_copy(c, k):
        peer = lax.rem(f + k, F)
        return pltpu.make_async_remote_copy(
            src_ref=tsend.at[c, peer], dst_ref=trecv[c].at[f],
            send_sem=t_s.at[c, k], recv_sem=t_r.at[c, k],
            device_id={"fsdp": peer}, device_id_type=MESH)

    def t_arrival(c, k):
        peer = lax.rem(f + F - k, F)
        return pltpu.make_async_remote_copy(
            src_ref=tsend.at[c, peer], dst_ref=trecv[c].at[peer],
            send_sem=t_s.at[c, k], recv_sem=t_r.at[c, k],
            device_id={"fsdp": peer}, device_id_type=MESH)

    factor = scale * math.sqrt(width)
    for c in range(C):
        product = dot(wb[...], nall[c].reshape(ff, cc))
        result = factor * (NEWTON_A * NEWTON_A * nall[c, r].astype(F32) + product)
        for b in range(F):
            tsend[c, b] = fold(result[b * q:(b + 1) * q]).astype(BF16)
        for k in range(1, F):
            t_copy(c, k).start()
        trecv[c][f] = tsend[c, f]

    for c in range(C):
        for k in range(1, F):
            t_arrival(c, k).wait_recv()
        for e in range(F):
            upd_ref[e, 0, :, cols(c)] = unfold(trecv[c][owners[e]].astype(F32)).astype(BF16)

    for c in range(C):
        for way in range(2):
            pos = position(way)
            for t in range(last):
                @pl.when(pos <= t)
                def _(c=c, way=way, t=t):
                    rs_copy(c, way, t).wait_send()

            @pl.when(pos < last)
            def _(c=c, way=way):
                own_copy(c, way).wait_send()

            for k in range(last - 1):
                @pl.when(jnp.logical_and(pos > k, pos < last))
                def _(c=c, way=way, k=k):
                    pass_copy(c, way, k).wait_send()
        for k in range(1, F):
            a_copy(c, k).wait_send()
            t_copy(c, k).wait_send()


def fused_step(grads, momentum, owner):
    Z, F = lax.axis_size("rep"), lax.axis_size("fsdp")
    q, width = momentum.shape[2], momentum.shape[3]
    C = CHUNKS
    cc = width // C
    rows = F * q
    ff = Z * rows
    vmem = pl.BlockSpec(memory_space=pltpu.VMEM)
    dma = pltpu.SemaphoreType.DMA
    any_place = pl.BlockSpec(memory_space=pl.ANY)
    updates, total = pl.pallas_call(
        functools.partial(step_kernel, Z, F, C),
        out_shape=(
            jax.ShapeDtypeStruct((F, 1, q, width), BF16),
            jax.ShapeDtypeStruct(momentum.shape, BF16),
        ),
        in_specs=[pl.BlockSpec(memory_space=pltpu.SMEM), any_place, any_place],
        out_specs=(vmem, vmem),
        scratch_shapes=[
            pltpu.VMEM((Z, rows, width), F32),
            pltpu.VMEM((2, C, Z - 1, rows, cc), BF16),
            pltpu.VMEM((2, C, Z - 1, rows, cc), BF16),
            pltpu.VMEM((C, F, 2 * q, cc // 2), BF16),
            pltpu.VMEM((C, F, 2 * q, cc // 2), BF16),
            pltpu.VMEM((C, Z, rows, cc), BF16),
            pltpu.VMEM((ff, ff), F32),
            pltpu.VMEM((ff, ff), BF16),
            pltpu.VMEM((ff, ff), BF16),
            pltpu.VMEM((ff, ff), BF16),
            pltpu.VMEM((rows, ff), BF16),
            pltpu.VMEM((C, F, 2 * q, cc // 2), BF16),
            dma((2, C, Z - 1)),
            dma((2, C, Z - 1)),
            dma((C, F)),
            dma((C, F)),
            dma((2, C, Z - 1)),
            dma((2, C, Z - 1)),
            dma((C, F)),
            dma((C, F)),
            pltpu.VMEM(momentum.shape, F32),
            dma((C + 1,)),
        ]
        + [pltpu.VMEM((F, 2 * q, cc // 2), BF16)] * C
        + [pltpu.VMEM(grads.shape[1:3] + (cc,), BF16)] * C,
        compiler_params=pltpu.CompilerParams(
            collective_id=0, has_side_effects=True, vmem_limit_bytes=58 * 1024 * 1024
        ),
        cost_estimate=pl.CostEstimate(
            flops=2 * ff * ff * width, bytes_accessed=16 * rows * width, transcendentals=0
        ),
    )(owner, grads, momentum)
    return updates, DECAY_RATE * momentum + total.astype(F32)


def finish_rows(own_gram, gram_matrix):
    squared = jnp.dot(own_gram, gram_matrix, preferred_element_type=jnp.float32)
    polynomial = (NEWTON_B * own_gram.astype(jnp.float32) + NEWTON_C * squared).astype(jnp.bfloat16)
    return polynomial


def rows_whole(current, first_row):
    slab_rows = current.shape[0]
    result = current.astype(jnp.float32)
    for iteration in range(ITERS):
        gathered = lax.all_gather(current, "rep", axis=0, tiled=True)
        if iteration == 0:
            values = gathered.astype(jnp.float32)
            frobenius = jnp.sqrt(jnp.sum(values * values))
            whole = (values / (frobenius + EPSILON)).astype(jnp.bfloat16)
            mine = lax.dynamic_slice_in_dim(whole, first_row, slab_rows, 0)
        else:
            whole = gathered
            mine = current
        gram_matrix = lax.dot_general(
            whole, whole, (((1,), (1,)), ((), ())), preferred_element_type=jnp.float32
        ).astype(jnp.bfloat16)
        own_gram = lax.dynamic_slice_in_dim(gram_matrix, first_row, slab_rows, 0)
        polynomial = finish_rows(own_gram, gram_matrix)
        result = NEWTON_A * mine.astype(jnp.float32) + jnp.dot(
            polynomial, whole, preferred_element_type=jnp.float32
        )
        current = result.astype(jnp.bfloat16)
    return result


def on_device(grads, momentum, owner):
    slots = lax.axis_size("fsdp")
    replica = lax.axis_index("rep")
    width = grads.shape[-1]
    terms = grads[0].astype(jnp.float32)
    summed = lax.psum_scatter(terms, "rep", scatter_dimension=1, tiled=True)
    onehot = (owner[:, None] == jnp.arange(slots, dtype=jnp.int32)[None, :]).astype(jnp.float32)
    outgoing = jnp.einsum("es,eqd->sqd", onehot, summed, precision=lax.Precision.HIGHEST)
    arrived = lax.all_to_all(outgoing, "fsdp", split_axis=0, concat_axis=1, tiled=True)
    grad_rows = arrived[0]
    moment = momentum[0].reshape(-1, width)
    moment_new = DECAY_RATE * moment + grad_rows
    nesterov = (grad_rows + DECAY_RATE * moment_new).astype(jnp.bfloat16)
    slab_rows = nesterov.shape[0]
    first_row = replica * slab_rows
    result = rows_whole(nesterov, first_row)
    factor = math.sqrt(width)
    update_rows = (factor * result).astype(jnp.bfloat16)
    returning = lax.all_to_all(
        update_rows.reshape(slots, slab_rows // slots, width),
        "fsdp",
        split_axis=0,
        concat_axis=0,
        tiled=True,
    )
    updates = jnp.einsum(
        "es,sqd->eqd", onehot.astype(jnp.bfloat16), returning, preferred_element_type=jnp.float32
    ).astype(jnp.bfloat16)
    return (updates[:, None], moment_new.reshape(1, slots, slab_rows // slots, width))


def step(grads, momentum, owner):
    Z, F = lax.axis_size("rep"), lax.axis_size("fsdp")
    q, width = momentum.shape[2], momentum.shape[3]
    if q % 8 == 0 and F % 2 == 0 and Z % 2 == 0 and Z > 2 and width % (256 * CHUNKS) == 0:
        return fused_step(grads, momentum, owner)
    return on_device(grads, momentum, owner)


def solution(mesh):
    placed = (P("rep", None, "fsdp", None), P("fsdp", None, "rep", None), P())
    return jax.shard_map(
        step,
        mesh=mesh,
        in_specs=placed,
        out_specs=(P(None, "fsdp", "rep", None), P("fsdp", None, "rep", None)),
        check_vma=False,
    )
```
